32 devices in a mesh: groups: 2 (over y), dp: 4 (over z), head: 2 (over x), sub: 2 (over core).
Axes of the slice: x: 2, y: 2, z: 4, core: 2. Of those that a mesh axis runs over, the one named last changes fastest.
Arguments:
- queries: bfloat16 [128, 64, 128], P(('groups', 'dp', 'sub'), 'head'), parts along dimension 0, may hold values from -8 to 8
- kv_cache: bfloat16 [8192, 8, 2, 16, 128], P(('groups', 'dp', 'sub'), 'head'), parts along dimension 0, may hold values from -8 to 8
- keep: int32 [128, 48], P(('groups', 'dp', 'sub')), parts along dimension 0, may hold values from 0 to 63, as said below
- lengths: int32 [128], P(('groups', 'dp', 'sub')), parts along dimension 0, may hold values from 384 to 768
- placement: int32 [128, 64], P(('groups', 'dp', 'sub')), parts along dimension 0, may hold values from 0 to 4095, as said below
- positions: int32 [128], P(('groups', 'dp', 'sub')), parts along dimension 0, may hold values from 0 to 4095
Outputs:
- attention: bfloat16 [128, 64, 128], P(('groups', 'dp', 'sub'), 'head'), parts along dimension 0
- log_norm: float32 [128, 64], P(('groups', 'dp', 'sub'), 'head'), parts along dimension 0
The draws below stay inside these ranges and needn't reach their ends.
There are 2 independent parts, one for each index of `groups`. The reference program is written for one: setup_inputs(seed, part) draws one part's arguments, and reference() takes and returns one part's arrays. A program takes and returns all parts, laid end to end along the dimension named above; each array names one. Nothing has to cross between parts.
Inputs may be any that keep to these rules, and one draw needn't show every extreme that they name: `keep`: each row holds distinct block numbers in increasing order. `placement`: every cache row is named once; the 8 requests of one device (aligned groups of 8 rows) have exactly 64 of their blocks in the cache rows of each device.
All inputs are finite; a program needn't handle non-finite values.
Results may differ from the reference program's by a relative error of at most 0.0058.
Values may be sent and summed in bfloat16 or wider, within the bound.
A program may use at most 128 MiB of HBM per device.

```python
import jax
import jax.numpy as jnp
from jax import lax

QH = 64
KVH = 8
HD = 128
BLK = 16
NBR = 64
KEEP = 48
OWNERS = 8
REQ = 64
POOL = 4096
SPREAD = 64


def draw_queries(key, part):
    first = jax.random.fold_in(key, 1)
    values = jnp.clip(jax.random.normal(first, (REQ, QH, HD), jnp.float32), -4.0, 4.0)
    return values.astype(jnp.bfloat16)


def draw_kv_cache(key, part):
    first = jax.random.fold_in(key, 2)
    second = jax.random.fold_in(key, 4)
    keys = jnp.clip(1.5 * jax.random.normal(first, (POOL, KVH, BLK, HD), jnp.float32), -6.0, 6.0)
    values = jnp.clip(jax.random.normal(second, (POOL, KVH, BLK, HD), jnp.float32), -4.0, 4.0)
    return jnp.stack([keys, values], axis=2).astype(jnp.bfloat16)


def draw_keep(key, part):
    row_keys = jax.random.split(jax.random.fold_in(key, 3), REQ)
    rows = jax.vmap(lambda one: jnp.sort(jax.random.permutation(one, NBR)[:KEEP]))(row_keys)
    return rows.astype(jnp.int32)


def draw_placement(key, part):
    pool_dev = OWNERS * SPREAD
    owner_keys = jax.random.split(jax.random.fold_in(key, 5), OWNERS)
    slot_order = jax.vmap(lambda one: jax.random.permutation(one, pool_dev))(owner_keys).astype(jnp.int32)
    offsets = (jnp.arange(OWNERS, dtype=jnp.int32) * pool_dev)[:, None, None]
    physical = (slot_order.reshape(OWNERS, OWNERS, SPREAD) + offsets).transpose(1, 0, 2).reshape(OWNERS, pool_dev)
    device_keys = jax.random.split(jax.random.fold_in(key, 7), OWNERS)
    order = jax.vmap(lambda one: jax.random.permutation(one, pool_dev))(device_keys).astype(jnp.int32)
    table = jax.vmap(lambda where_to, what: jnp.zeros((pool_dev,), jnp.int32).at[where_to].set(what))(order, physical)
    return table.reshape(REQ, NBR).astype(jnp.int32)


def place_ends(values, stream_key, low, top_value):
    index_at = [jax.random.randint(jax.random.fold_in(stream_key, axis), (), 0, length) for axis, length in enumerate(values.shape)]
    widest = values.shape.index(max(values.shape))
    next_to = index_at[:widest] + [(index_at[widest] + 1) % values.shape[widest]] + index_at[widest + 1:]
    return values.at[tuple(index_at)].set(low).at[tuple(next_to)].set(top_value)


def setup_inputs(seed: int = 0, part: int = 0) -> dict:
    arg_keys = jax.random.split(jax.random.key(seed), 7)
    part_splits = jax.random.split(jax.random.fold_in(arg_keys[6], part), 7)
    queries = draw_queries(jax.random.fold_in(jax.random.fold_in(arg_keys[6], part), 71), part)
    kv_cache = draw_kv_cache(jax.random.fold_in(jax.random.fold_in(arg_keys[6], part), 71), part)
    keep = draw_keep(jax.random.fold_in(jax.random.fold_in(arg_keys[6], part), 71), part)
    lengths = place_ends(jax.random.randint(part_splits[3], (REQ,), KEEP * BLK // 2, KEEP * BLK + 1), jax.random.fold_in(part_splits[3], 1), KEEP * BLK // 2, KEEP * BLK).astype(jnp.int32)
    placement = draw_placement(jax.random.fold_in(jax.random.fold_in(arg_keys[6], part), 71), part)
    positions = place_ends(jax.random.randint(part_splits[5], (REQ,), 0, 4096), jax.random.fold_in(part_splits[5], 1), 0, 4095).astype(jnp.int32)
    return dict(queries=queries, kv_cache=kv_cache, keep=keep, lengths=lengths, placement=placement, positions=positions)


def rotate(values, positions):
    half = values.shape[-1] // 2
    inverse = 1000000.0 ** (-(2.0 * jnp.arange(half, dtype=jnp.float32)) / values.shape[-1])
    angle = positions.astype(jnp.float32)[:, None] * inverse[None, :]
    cosine = jnp.cos(angle)[:, None, :]
    sine = jnp.sin(angle)[:, None, :]
    first = values[..., :half]
    second = values[..., half:]
    return jnp.concatenate([first * cosine - second * sine, second * cosine + first * sine], axis=-1)


def reference(queries, kv_cache, keep, lengths, placement, positions):
    group = QH // KVH
    factor = HD ** -0.5
    rotated = rotate(queries.astype(jnp.float32), positions).astype(jnp.bfloat16)

    def single(items):
        query, kept, length, table = items
        rows = jnp.take(table, kept).astype(jnp.int32)
        blocks = jnp.take(kv_cache, rows, axis=0)
        keys = blocks[:, :, 0].astype(jnp.float32)
        values = blocks[:, :, 1].astype(jnp.float32)
        grouped = query.reshape(KVH, group, HD).astype(jnp.float32)
        scores = jnp.einsum("kgd,bktd->bkgt", grouped, keys) * factor
        tokens = jnp.arange(KEEP, dtype=jnp.int32)[:, None] * BLK + jnp.arange(BLK, dtype=jnp.int32)[None, :]
        live = (tokens < length)[:, None, None, :]
        peak = jnp.max(jnp.where(live, scores, -1e30), axis=-1)
        weights = jnp.where(live, jnp.exp(scores - peak[..., None]), 0.0).astype(jnp.bfloat16)
        totals = jnp.sum(weights.astype(jnp.float32), axis=-1)
        partial_value = jnp.einsum("bkgt,bktd->bkgd", weights.astype(jnp.float32), values)
        top = jnp.max(peak, axis=0)
        scale = jnp.exp(peak - top[None])
        norm = jnp.sum(scale * totals, axis=0)
        merged = jnp.einsum("bkg,bkgd->kgd", scale, partial_value, precision=lax.Precision.HIGHEST)
        output = (merged / norm[..., None]).reshape(QH, HD).astype(jnp.bfloat16)
        return output, (top + jnp.log(norm)).reshape(QH)

    attention, log_norm = lax.map(single, (rotated, keep, lengths, placement))
    return attention, log_norm
```

```python
from functools import partial
import math

import jax
import jax.numpy as jnp
import numpy as np
from jax import lax
from jax.experimental import pallas as pl
from jax.experimental.pallas import tpu as pltpu
from jax.sharding import PartitionSpec as P

MESH = pl.DeviceIdType.MESH
DEAD = -1e30
CHUNKS = 8
F32 = jnp.float32
BF16 = jnp.bfloat16
I32 = jnp.int32


def dot_lanes(a, b):
    return lax.dot_general(a, b, (((1,), (1,)), ((), ())), preferred_element_type=F32)


def iota(shape, axis):
    return lax.broadcasted_iota(I32, shape, axis)


def kernel(
    chips, subs, pos_ref, len_ref, freq_ref, q_ref, keep_ref, place_ref, kv_ref,
    att_ref, log_ref,
    kv, qall, meta_send, meta_recv, meta_s, live_of, own, sib_send, sib_recv, z_send, z_recv, zs_send, zs_recv,
    kv_sem, meta_ssem, meta_rsem, smem_sem, q_ssem, q_rsem, relay_ssem, sib_ssem, sib_rsem,
    z_ssem, z_rsem, zs_ssem, zs_rsem,
):
    owners = chips * subs
    requests, q_heads, head_dim = q_ref.shape
    pool, kv_heads, _, block_len, _ = kv_ref.shape
    group = q_heads // kv_heads
    blocks = place_ref.shape[1]
    kept = keep_ref.shape[1]
    spread = pool // owners
    rows_q = requests * group
    half = head_dim // 2
    scale = head_dim ** -0.5 * math.log2(math.e)
    shift = pool.bit_length() - 1
    my_chip = lax.axis_index("dp")
    my_sub = lax.axis_index("sub")
    me = my_chip * subs + my_sub
    other = 1 - my_sub

    def place(o):
        return {"dp": o // subs, "sub": lax.rem(o, subs)}

    def kv_copy(i):
        part = pl.ds(i * (pool // CHUNKS), pool // CHUNKS)
        return pltpu.make_async_copy(kv_ref.at[part], kv.at[part], kv_sem.at[i])

    def meta_copy(o, slot):
        return pltpu.make_async_remote_copy(
            src_ref=meta_send.at[o], dst_ref=meta_recv.at[slot], send_sem=meta_ssem.at[o],
            recv_sem=meta_rsem.at[slot], device_id=place(o), device_id_type=MESH)

    def q_copy(to, slot, ssem):
        return pltpu.make_async_remote_copy(
            src_ref=qall.at[slot], dst_ref=qall.at[slot], send_sem=ssem,
            recv_sem=q_rsem.at[slot], device_id=place(to), device_id_type=MESH)

    def sib_copy(t):
        return pltpu.make_async_remote_copy(
            src_ref=sib_send.at[t], dst_ref=sib_recv.at[t], send_sem=sib_ssem.at[t],
            recv_sem=sib_rsem.at[t], device_id=place(my_chip * subs + other), device_id_type=MESH)

    def z_copies(t, chip, slot):
        to = place(chip * subs + my_sub)
        return (
            pltpu.make_async_remote_copy(
                src_ref=z_send.at[t], dst_ref=z_recv.at[slot], send_sem=z_ssem.at[t],
                recv_sem=z_rsem.at[slot], device_id=to, device_id_type=MESH),
            pltpu.make_async_remote_copy(
                src_ref=zs_send.at[t], dst_ref=zs_recv.at[slot], send_sem=zs_ssem.at[t],
                recv_sem=zs_rsem.at[slot], device_id=to, device_id_type=MESH),
        )

    barrier = pltpu.get_barrier_semaphore()

    @pl.loop(1, owners)
    def _(i):
        pl.semaphore_signal(barrier, inc=1, device_id=place(lax.rem(me + i, owners)), device_id_type=MESH)

    for i in range(CHUNKS):
        kv_copy(i).start()

    row = iota((requests, 1), 0)
    positions = jnp.zeros((requests, 1), F32)
    for r in range(requests):
        positions = jnp.where(row == r, pos_ref[r].astype(F32), positions)
    angle = positions * freq_ref[...]
    cosine, sine = jnp.cos(angle)[:, None, :], jnp.sin(angle)[:, None, :]
    values = q_ref[...].astype(F32)
    first, second = values[..., :half], values[..., half:]
    rotated = jnp.concatenate([first * cosine - second * sine, second * cosine + first * sine], axis=-1)
    for k in range(kv_heads):
        qall[me, k] = rotated[:, k * group:(k + 1) * group, :].reshape(rows_q, head_dim).astype(BF16)

    table = place_ref[...]
    owner_of = lax.shift_right_logical(table, shift)
    local_of = table & (pool - 1)
    low, high = (local_of & 255).astype(F32), lax.shift_right_logical(local_of, 8).astype(F32)
    member = [
        (owner_of[r:r + 1] == iota((owners, blocks), 0)).astype(F32) for r in range(requests)
    ]
    before = (iota((blocks, blocks), 0) < iota((blocks, blocks), 1)).astype(F32).astype(BF16)
    ranks = jnp.dot(jnp.concatenate(member, 0).astype(BF16), before, preferred_element_type=F32)
    base = jnp.zeros((owners, 1), F32)
    fields = jnp.zeros((3 * owners, spread), F32)
    for r in range(requests):
        m = member[r]
        rank = jnp.sum(m * (ranks[r * owners:(r + 1) * owners] + base), axis=0, keepdims=True)
        base = base + jnp.sum(m, axis=1, keepdims=True)
        at = (rank.astype(I32) == iota((spread, blocks), 0)).astype(F32).astype(BF16)
        named = (keep_ref[r:r + 1, :] == iota((blocks, kept), 0)).astype(F32).astype(BF16)
        live = jnp.clip(len_ref[r] - iota((8, kept), 1) * block_len, 0, block_len)
        count = dot_lanes(live.astype(F32).astype(BF16), named)[:1]
        code = count + float(r * (block_len + 1))
        stacked = jnp.concatenate([m * low[r:r + 1], m * high[r:r + 1], m * code], 0)
        fields = fields + dot_lanes(stacked.astype(BF16), at)
    ids = (fields[:owners] + 256.0 * fields[owners:2 * owners]).astype(I32)
    codes = fields[2 * owners:].astype(I32)
    meta_send[...] = jnp.zeros_like(meta_send)
    for o in range(owners):
        meta_send[o, 0:1, 0:spread] = ids[o:o + 1]
        meta_send[o, 1:2, 0:spread] = codes[o:o + 1]
    meta_recv[me] = meta_send[me]

    pl.semaphore_wait(barrier, owners - 1)

    @pl.loop(1, owners)
    def _(i):
        o = lax.rem(me + i, owners)
        meta_copy(o, me).start()

    @pl.loop(1, chips)
    def _(t):
        chip = lax.rem(my_chip + t, chips)
        q_copy(chip * subs + my_sub, me, q_ssem.at[t]).start()

    q_copy(my_chip * subs + other, me, q_ssem.at[0]).start()

    @pl.loop(1, owners)
    def _(i):
        o = lax.rem(me + i, owners)
        meta_copy(o, o).wait_recv()

    to_smem = pltpu.make_async_copy(meta_recv, meta_s, smem_sem)
    to_smem.start()
    keys = spread * block_len
    expand = (lax.shift_right_logical(iota((spread, keys), 1), block_len.bit_length() - 1)
              == iota((spread, keys), 0)).astype(F32).astype(BF16)
    wide = jnp.dot(meta_recv[:, 1, 0:spread].astype(F32).astype(BF16), expand, preferred_element_type=F32)
    request = jnp.floor((wide + 0.5) * (1.0 / (block_len + 1)))
    count = wide - request * (block_len + 1)
    token = (iota((owners, keys), 1) & (block_len - 1)).astype(F32)
    live_of[...] = jnp.where(token < count, request, -1.0)
    to_smem.wait()
    for i in range(CHUNKS):
        kv_copy(i).wait()

    lane = iota((rows_q, head_dim), 1)

    def attend(o, out):
        wanted = live_of[pl.ds(o, 1), :]
        wanted = jnp.broadcast_to(wanted, (group, keys))
        ids = [meta_s[o, 0, j] & (pool - 1) for j in range(spread)]
        stats = jnp.zeros((rows_q, head_dim), F32)
        for k in range(kv_heads):
            key = jnp.concatenate([kv[ids[j], k, 0] for j in range(spread)], 0)
            value = jnp.concatenate([kv[ids[j], k, 1] for j in range(spread)], 0)
            score = dot_lanes(qall[o, k], key)
            score = jnp.concatenate(
                [jnp.where(wanted == float(r), score[r * group:(r + 1) * group], DEAD) for r in range(requests)], 0)
            peak = jnp.max(score, axis=1, keepdims=True)
            weight = jnp.exp2((score - peak) * scale).astype(BF16)
            total = jnp.sum(weight.astype(F32), axis=1, keepdims=True)
            out[k] = jnp.dot(weight, value, preferred_element_type=F32)
            stats = jnp.where(lane == k, peak, stats)
            stats = jnp.where(lane == kv_heads + k, total, stats)
        out[kv_heads] = stats

    def merge(t):
        a, b = own[t, kv_heads], sib_recv[t, kv_heads]
        stats = jnp.zeros((rows_q, head_dim), F32)
        for k in range(kv_heads):
            ma, mb = a[:, k:k + 1], b[:, k:k + 1]
            la, lb = a[:, kv_heads + k:kv_heads + k + 1], b[:, kv_heads + k:kv_heads + k + 1]
            peak = jnp.maximum(ma, mb)
            wa, wb = jnp.exp2((ma - peak) * scale), jnp.exp2((mb - peak) * scale)
            own[t, k] = own[t, k] * wa + sib_recv[t, k] * wb
            stats = jnp.where(lane == k, peak, stats)
            stats = jnp.where(lane == kv_heads + k, la * wa + lb * wb, stats)
        own[t, kv_heads] = stats

    def send_back(t):
        sib_copy(t).wait_recv()
        merge(t)
        for k in range(kv_heads):
            z_send[t, k] = own[t, k].astype(BF16)
        zs_send[t] = jnp.transpose(own[t, kv_heads])[:2 * kv_heads]
        for copy in z_copies(t, lax.rem(my_chip + t, chips), my_chip):
            copy.start()

    @pl.loop(1, chips + 1)
    def _(i):
        t = lax.rem(i, chips)
        chip = lax.rem(my_chip + t, chips)
        mine, sibs = chip * subs + my_sub, chip * subs + other

        @pl.when(t > 0)
        def _():
            q_copy(my_chip * subs + other, mine, relay_ssem.at[t]).wait_recv()
            q_copy(my_chip * subs + other, mine, relay_ssem.at[t]).start()

        attend(mine, own.at[t])
        q_copy(my_chip * subs + other, sibs, relay_ssem.at[t]).wait_recv()
        attend(sibs, sib_send.at[t])
        sib_copy(t).start()

        @pl.when(i > 1)
        def _():
            send_back(i - 1)

    sib_copy(0).wait_recv()
    merge(0)

    @pl.loop(1, chips)
    def _(t):
        chip = lax.rem(my_chip + t, chips)
        for copy in z_copies(t, chip, chip):
            copy.wait_recv()
        pad = jnp.zeros((head_dim - 2 * kv_heads, rows_q), F32)
        b = jnp.transpose(jnp.concatenate([zs_recv[chip], pad], 0))
        a = own[0, kv_heads]
        stats = jnp.zeros((rows_q, head_dim), F32)
        for k in range(kv_heads):
            ma, mb = a[:, k:k + 1], b[:, k:k + 1]
            la, lb = a[:, kv_heads + k:kv_heads + k + 1], b[:, kv_heads + k:kv_heads + k + 1]
            peak = jnp.maximum(ma, mb)
            wa, wb = jnp.exp2((ma - peak) * scale), jnp.exp2((mb - peak) * scale)
            own[0, k] = own[0, k] * wa + z_recv[chip, k].astype(F32) * wb
            stats = jnp.where(lane == k, peak, stats)
            stats = jnp.where(lane == kv_heads + k, la * wa + lb * wb, stats)
        own[0, kv_heads] = stats

    stats = own[0, kv_heads]
    outs = []
    spot = iota((rows_q, q_heads), 1)
    turn = iota((rows_q, q_heads), 0) & (group - 1)
    logs = jnp.zeros((rows_q, q_heads), F32)
    for k in range(kv_heads):
        norm = stats[:, kv_heads + k:kv_heads + k + 1]
        outs.append((own[0, k] / norm).reshape(requests, group, head_dim))
        value = stats[:, k:k + 1] * (head_dim ** -0.5) + jnp.log(norm)
        logs = jnp.where(spot == turn + k * group, value, logs)
    att_ref[...] = jnp.concatenate(outs, 1).astype(BF16)
    log_ref[...] = jnp.sum(logs.reshape(requests, group, q_heads), axis=1)

    @pl.loop(1, owners)
    def _(i):
        meta_copy(lax.rem(me + i, owners), me).wait_send()

    @pl.loop(0, chips)
    def _(t):
        q_copy(my_chip * subs + other, me, q_ssem.at[t]).wait_send()
        sib_copy(t).wait_send()

    @pl.loop(1, chips)
    def _(t):
        chip = lax.rem(my_chip + t, chips)
        q_copy(my_chip * subs + other, chip * subs + my_sub, relay_ssem.at[t]).wait_send()
        for copy in z_copies(t, chip, my_chip):
            copy.wait_send()


def local(queries, kv_cache, keep, lengths, placement, positions):
    chips, subs = lax.axis_size("dp"), lax.axis_size("sub")
    owners = chips * subs
    requests, q_heads, head_dim = queries.shape
    pool, kv_heads, _, block_len, _ = kv_cache.shape
    spread = pool // owners
    group = q_heads // kv_heads
    rows_q = requests * group
    assert subs == 2 and pool & (pool - 1) == 0 and pool <= 65536
    assert requests * (block_len + 1) <= 256 and block_len & (block_len - 1) == 0
    assert 2 * kv_heads <= head_dim and group & (group - 1) == 0 and spread <= 128
    half = head_dim // 2
    freq = jnp.asarray(
        (1000000.0 ** (-(2.0 * np.arange(half, dtype=np.float64)) / head_dim)).astype(np.float32)[None])
    vmem, smem = pl.BlockSpec(memory_space=pltpu.VMEM), pl.BlockSpec(memory_space=pltpu.SMEM)
    dma = pltpu.SemaphoreType.DMA
    part = (chips, kv_heads + 1, rows_q, head_dim)
    return pl.pallas_call(
        partial(kernel, chips, subs),
        out_shape=(
            jax.ShapeDtypeStruct(queries.shape, BF16),
            jax.ShapeDtypeStruct((requests, q_heads), F32),
        ),
        in_specs=[smem, smem, vmem, vmem, vmem, vmem, pl.BlockSpec(memory_space=pl.ANY)],
        out_specs=(vmem, vmem),
        scratch_shapes=[
            pltpu.VMEM(kv_cache.shape, BF16),
            pltpu.VMEM((owners, kv_heads, rows_q, head_dim), BF16),
            pltpu.VMEM((owners, 8, 128), I32),
            pltpu.VMEM((owners, 8, 128), I32),
            pltpu.SMEM((owners, 8, 128), I32),
            pltpu.VMEM((owners, spread * block_len), F32),
            pltpu.VMEM(part, F32),
            pltpu.VMEM(part, F32),
            pltpu.VMEM(part, F32),
            pltpu.VMEM((chips, kv_heads, rows_q, head_dim), BF16),
            pltpu.VMEM((chips, kv_heads, rows_q, head_dim), BF16),
            pltpu.VMEM((chips, 2 * kv_heads, rows_q), F32),
            pltpu.VMEM((chips, 2 * kv_heads, rows_q), F32),
            dma((CHUNKS,)), dma((owners,)), dma((owners,)), dma,
            dma((chips,)), dma((owners,)), dma((chips,)), dma((chips,)), dma((chips,)),
            dma((chips,)), dma((chips,)), dma((chips,)), dma((chips,)),
        ],
        compiler_params=pltpu.CompilerParams(
            collective_id=0, has_side_effects=True, vmem_limit_bytes=48 * 2 ** 20),
        name="paged",
    )(positions, lengths, freq, queries, keep, placement, kv_cache)


def solution(mesh):
    in_specs = (
        P(("groups", "dp", "sub"), "head", None),
        P(("groups", "dp", "sub"), "head", None, None, None),
        P(("groups", "dp", "sub"), None),
        P(("groups", "dp", "sub")),
        P(("groups", "dp", "sub"), None),
        P(("groups", "dp", "sub")),
    )
    out_specs = (P(("groups", "dp", "sub"), "head", None), P(("groups", "dp", "sub"), "head"))
    return jax.shard_map(local, mesh=mesh, in_specs=in_specs, out_specs=out_specs, check_vma=False)
```

```python
from functools import partial
import math

import jax
import jax.numpy as jnp
import numpy as np
from jax import lax
from jax.experimental import pallas as pl
from jax.experimental.pallas import tpu as pltpu
from jax.sharding import PartitionSpec as P

MESH = pl.DeviceIdType.MESH
DEAD = -1e30
CHUNKS = 8
F32 = jnp.float32
BF16 = jnp.bfloat16
I32 = jnp.int32


def dot_lanes(a, b):
    return lax.dot_general(a, b, (((1,), (1,)), ((), ())), preferred_element_type=F32)


def iota(shape, axis):
    return lax.broadcasted_iota(I32, shape, axis)


def kernel(
    chips, subs, pos_hbm, len_hbm, q_hbm, keep_hbm, place_hbm, kv_ref,
    att_ref, log_ref,
    pos_ref, len_ref, q_ref, keep_ref, place_ref, in_sem, own_s, own_live, own_sem, kv, qall, meta_send, meta_recv, meta_s, live_of, own, sib_send, sib_recv, z_send, z_recv, zs_send, zs_recv,
    kv_sem, meta_ssem, meta_rsem, smem_sem, q_ssem, q_rsem, relay_ssem, sib_ssem, sib_rsem,
    z_ssem, z_rsem, zs_ssem, zs_rsem,
):
    owners = chips * subs
    requests, q_heads, head_dim = q_ref.shape
    pool, kv_heads, _, block_len, _ = kv_ref.shape
    group = q_heads // kv_heads
    blocks = place_ref.shape[1]
    kept = keep_ref.shape[1]
    spread = pool // owners
    rows_q = requests * group
    half = head_dim // 2
    scale = head_dim ** -0.5 * math.log2(math.e)
    shift = pool.bit_length() - 1
    my_chip = lax.axis_index("dp")
    my_sub = lax.axis_index("sub")
    me = my_chip * subs + my_sub
    other = 1 - my_sub

    def place(o):
        return {"dp": o // subs, "sub": lax.rem(o, subs)}

    def kv_copy(i):
        part = pl.ds(i * (pool // CHUNKS), pool // CHUNKS)
        return pltpu.make_async_copy(kv_ref.at[part], kv.at[part], kv_sem.at[i])

    def meta_copy(o, slot):
        return pltpu.make_async_remote_copy(
            src_ref=meta_send.at[o], dst_ref=meta_recv.at[slot], send_sem=meta_ssem.at[o],
            recv_sem=meta_rsem.at[slot], device_id=place(o), device_id_type=MESH)

    def q_copy(to, slot, ssem):
        return pltpu.make_async_remote_copy(
            src_ref=qall.at[slot], dst_ref=qall.at[slot], send_sem=ssem,
            recv_sem=q_rsem.at[slot], device_id=place(to), device_id_type=MESH)

    def sib_copy(t):
        return pltpu.make_async_remote_copy(
            src_ref=sib_send.at[t], dst_ref=sib_recv.at[t], send_sem=sib_ssem.at[t],
            recv_sem=sib_rsem.at[t], device_id=place(my_chip * subs + other), device_id_type=MESH)

    def z_copies(t, chip, slot):
        to = place(chip * subs + my_sub)
        return (
            pltpu.make_async_remote_copy(
                src_ref=z_send.at[t], dst_ref=z_recv.at[slot], send_sem=z_ssem.at[t],
                recv_sem=z_rsem.at[slot], device_id=to, device_id_type=MESH),
            pltpu.make_async_remote_copy(
                src_ref=zs_send.at[t], dst_ref=zs_recv.at[slot], send_sem=zs_ssem.at[t],
                recv_sem=zs_rsem.at[slot], device_id=to, device_id_type=MESH),
        )

    inputs = [
        pltpu.make_async_copy(source, here, in_sem.at[i])
        for i, (source, here) in enumerate((
            (place_hbm, place_ref), (keep_hbm, keep_ref), (len_hbm, len_ref), (pos_hbm, pos_ref), (q_hbm, q_ref)))
    ]
    for copy in inputs:
        copy.start()

    barrier = pltpu.get_barrier_semaphore()

    @pl.loop(1, owners)
    def _(i):
        pl.semaphore_signal(barrier, inc=1, device_id=place(lax.rem(me + i, owners)), device_id_type=MESH)

    for i in range(CHUNKS):
        kv_copy(i).start()

    for copy in inputs:
        copy.wait()

    row = iota((requests, 1), 0)
    positions = jnp.zeros((requests, 1), F32)
    for r in range(requests):
        positions = jnp.where(row == r, pos_ref[r].astype(F32), positions)
    place_i = iota((1, half), 1)
    freq = jnp.ones((1, half), F32)
    for bit in range(half.bit_length() - 1):
        step = float(np.float32(1000000.0 ** (-2.0 * 2 ** bit / head_dim)))
        freq = freq * jnp.where((place_i & (1 << bit)) != 0, step, 1.0)
    angle = positions * freq
    cosine, sine = jnp.cos(angle)[:, None, :], jnp.sin(angle)[:, None, :]
    values = q_ref[...].astype(F32)
    first, second = values[..., :half], values[..., half:]
    rotated = jnp.concatenate([first * cosine - second * sine, second * cosine + first * sine], axis=-1)
    for k in range(kv_heads):
        qall[me, k] = rotated[:, k * group:(k + 1) * group, :].reshape(rows_q, head_dim).astype(BF16)

    table = place_ref[...]
    owner_of = lax.shift_right_logical(table, shift)
    local_of = table & (pool - 1)
    low, high = (local_of & 255).astype(F32), lax.shift_right_logical(local_of, 8).astype(F32)
    member = [
        (owner_of[r:r + 1] == iota((owners, blocks), 0)).astype(F32) for r in range(requests)
    ]
    before = (iota((blocks, blocks), 0) < iota((blocks, blocks), 1)).astype(F32).astype(BF16)
    ranks = jnp.dot(jnp.concatenate(member, 0).astype(BF16), before, preferred_element_type=F32)
    base = jnp.zeros((owners, 1), F32)
    fields = jnp.zeros((3 * owners, spread), F32)
    for r in range(requests):
        m = member[r]
        rank = jnp.sum(m * (ranks[r * owners:(r + 1) * owners] + base), axis=0, keepdims=True)
        base = base + jnp.sum(m, axis=1, keepdims=True)
        at = (rank.astype(I32) == iota((spread, blocks), 0)).astype(F32).astype(BF16)
        named = (keep_ref[r:r + 1, :] == iota((blocks, kept), 0)).astype(F32).astype(BF16)
        live = jnp.clip(len_ref[r] - iota((8, kept), 1) * block_len, 0, block_len)
        count = dot_lanes(live.astype(F32).astype(BF16), named)[:1]
        code = count + float(r * (block_len + 1))
        stacked = jnp.concatenate([m * low[r:r + 1], m * high[r:r + 1], m * code], 0)
        fields = fields + dot_lanes(stacked.astype(BF16), at)
    ids = (fields[:owners] + 256.0 * fields[owners:2 * owners]).astype(I32)
    codes = fields[2 * owners:].astype(I32)
    meta_send[...] = jnp.zeros_like(meta_send)
    for o in range(owners):
        meta_send[o, 0:1, 0:spread] = ids[o:o + 1]
        meta_send[o, 1:2, 0:spread] = codes[o:o + 1]
    meta_recv[me] = meta_send[me]

    own_smem = pltpu.make_async_copy(meta_send.at[me], own_s, own_sem)
    own_smem.start()
    keys = spread * block_len
    expand = (lax.shift_right_logical(iota((spread, keys), 1), block_len.bit_length() - 1)
              == iota((spread, keys), 0)).astype(F32).astype(BF16)

    def live_requests(codes):
        wide = jnp.dot(codes.astype(F32).astype(BF16), expand, preferred_element_type=F32)
        request = jnp.floor((wide + 0.5) * (1.0 / (block_len + 1)))
        count = wide - request * (block_len + 1)
        token = (iota(wide.shape, 1) & (block_len - 1)).astype(F32)
        return jnp.where(token < count, request, -1.0)

    own_live[...] = live_requests(jnp.broadcast_to(meta_send[me, 1:2, 0:spread], (8, spread)))
    own_smem.wait()

    pl.semaphore_wait(barrier, owners - 1)

    @pl.loop(1, owners)
    def _(i):
        o = lax.rem(me + i, owners)
        meta_copy(o, me).start()

    q_copy(my_chip * subs + other, me, q_ssem.at[0]).start()

    @pl.loop(1, chips)
    def _(t):
        chip = lax.rem(my_chip + t, chips)
        q_copy(chip * subs + my_sub, me, q_ssem.at[t]).start()

    for i in range(CHUNKS):
        kv_copy(i).wait()

    lane = iota((rows_q, head_dim), 1)

    def attend(o, live, rows, out):
        wanted = jnp.broadcast_to(live, (group, keys))
        ids = [rows[0, j] & (pool - 1) for j in range(spread)]
        stats = jnp.zeros((rows_q, head_dim), F32)
        for k in range(kv_heads):
            key = jnp.concatenate([kv[ids[j], k, 0] for j in range(spread)], 0)
            value = jnp.concatenate([kv[ids[j], k, 1] for j in range(spread)], 0)
            score = dot_lanes(qall[o, k], key)
            score = jnp.concatenate(
                [jnp.where(wanted == float(r), score[r * group:(r + 1) * group], DEAD) for r in range(requests)], 0)
            peak = jnp.max(score, axis=1, keepdims=True)
            weight = jnp.exp2((score - peak) * scale).astype(BF16)
            total = jnp.sum(weight.astype(F32), axis=1, keepdims=True)
            out[k] = jnp.dot(weight, value, preferred_element_type=F32)
            stats = jnp.where(lane == k, peak, stats)
            stats = jnp.where(lane == kv_heads + k, total, stats)
        out[kv_heads] = stats

    def merge(t):
        a, b = own[t, kv_heads], sib_recv[t, kv_heads]
        stats = jnp.zeros((rows_q, head_dim), F32)
        for k in range(kv_heads):
            ma, mb = a[:, k:k + 1], b[:, k:k + 1]
            la, lb = a[:, kv_heads + k:kv_heads + k + 1], b[:, kv_heads + k:kv_heads + k + 1]
            peak = jnp.maximum(ma, mb)
            wa, wb = jnp.exp2((ma - peak) * scale), jnp.exp2((mb - peak) * scale)
            own[t, k] = own[t, k] * wa + sib_recv[t, k] * wb
            stats = jnp.where(lane == k, peak, stats)
            stats = jnp.where(lane == kv_heads + k, la * wa + lb * wb, stats)
        own[t, kv_heads] = stats

    def send_back(t):
        sib_copy(t).wait_recv()
        merge(t)
        for k in range(kv_heads):
            z_send[t, k] = own[t, k].astype(BF16)
        zs_send[t] = jnp.transpose(own[t, kv_heads])[:2 * kv_heads]
        for copy in z_copies(t, lax.rem(my_chip + t, chips), my_chip):
            copy.start()

    attend(me, own_live[0:1, :], own_s, own.at[0])

    @pl.loop(1, owners)
    def _(i):
        o = lax.rem(me + i, owners)
        meta_copy(o, o).wait_recv()

    to_smem = pltpu.make_async_copy(meta_recv, meta_s, smem_sem)
    to_smem.start()
    live_of[...] = live_requests(meta_recv[:, 1, 0:spread])
    to_smem.wait()

    @pl.loop(0, chips)
    def _(t):
        chip = lax.rem(my_chip + t, chips)
        mine, sibs = chip * subs + my_sub, chip * subs + other

        @pl.when(t < chips - 1)
        def _():
            ahead = lax.rem(my_chip + t + 1, chips) * subs + my_sub
            relay = q_copy(my_chip * subs + other, ahead, relay_ssem.at[t + 1])
            relay.wait_recv()
            relay.start()

        q_copy(my_chip * subs + other, sibs, relay_ssem.at[t]).wait_recv()
        attend(sibs, live_of[pl.ds(sibs, 1), :], meta_s.at[sibs], sib_send.at[t])
        sib_copy(t).start()

        @pl.when(t > 0)
        def _():
            attend(mine, live_of[pl.ds(mine, 1), :], meta_s.at[mine], own.at[t])
            send_back(t)

    sib_copy(0).wait_recv()
    merge(0)

    @pl.loop(1, chips)
    def _(t):
        chip = lax.rem(my_chip + chips - t, chips)
        for copy in z_copies(t, chip, chip):
            copy.wait_recv()
        pad = jnp.zeros((head_dim - 2 * kv_heads, rows_q), F32)
        b = jnp.transpose(jnp.concatenate([zs_recv[chip], pad], 0))
        a = own[0, kv_heads]
        stats = jnp.zeros((rows_q, head_dim), F32)
        for k in range(kv_heads):
            ma, mb = a[:, k:k + 1], b[:, k:k + 1]
            la, lb = a[:, kv_heads + k:kv_heads + k + 1], b[:, kv_heads + k:kv_heads + k + 1]
            peak = jnp.maximum(ma, mb)
            wa, wb = jnp.exp2((ma - peak) * scale), jnp.exp2((mb - peak) * scale)
            own[0, k] = own[0, k] * wa + z_recv[chip, k].astype(F32) * wb
            stats = jnp.where(lane == k, peak, stats)
            stats = jnp.where(lane == kv_heads + k, la * wa + lb * wb, stats)
        own[0, kv_heads] = stats

    stats = own[0, kv_heads]
    outs = []
    spot = iota((rows_q, q_heads), 1)
    turn = iota((rows_q, q_heads), 0) & (group - 1)
    logs = jnp.zeros((rows_q, q_heads), F32)
    for k in range(kv_heads):
        norm = stats[:, kv_heads + k:kv_heads + k + 1]
        outs.append((own[0, k] / norm).reshape(requests, group, head_dim))
        value = stats[:, k:k + 1] * (head_dim ** -0.5) + jnp.log(norm)
        logs = jnp.where(spot == turn + k * group, value, logs)
    att_ref[...] = jnp.concatenate(outs, 1).astype(BF16)
    log_ref[...] = jnp.sum(logs.reshape(requests, group, q_heads), axis=1)

    @pl.loop(1, owners)
    def _(i):
        meta_copy(lax.rem(me + i, owners), me).wait_send()

    @pl.loop(0, chips)
    def _(t):
        q_copy(my_chip * subs + other, me, q_ssem.at[t]).wait_send()
        sib_copy(t).wait_send()

    @pl.loop(1, chips)
    def _(t):
        chip = lax.rem(my_chip + t, chips)
        q_copy(my_chip * subs + other, chip * subs + my_sub, relay_ssem.at[t]).wait_send()
        for copy in z_copies(t, chip, my_chip):
            copy.wait_send()


def local(queries, kv_cache, keep, lengths, placement, positions):
    chips, subs = lax.axis_size("dp"), lax.axis_size("sub")
    owners = chips * subs
    requests, q_heads, head_dim = queries.shape
    pool, kv_heads, _, block_len, _ = kv_cache.shape
    spread = pool // owners
    group = q_heads // kv_heads
    rows_q = requests * group
    assert head_dim & (head_dim - 1) == 0
    assert subs == 2 and pool & (pool - 1) == 0 and pool <= 65536
    assert requests * (block_len + 1) <= 256 and block_len & (block_len - 1) == 0
    assert 2 * kv_heads <= head_dim and group & (group - 1) == 0 and spread <= 128
    vmem, hbm = pl.BlockSpec(memory_space=pltpu.VMEM), pl.BlockSpec(memory_space=pltpu.HBM)
    dma = pltpu.SemaphoreType.DMA
    part = (chips, kv_heads + 1, rows_q, head_dim)
    return pl.pallas_call(
        partial(kernel, chips, subs),
        out_shape=(
            jax.ShapeDtypeStruct(queries.shape, BF16),
            jax.ShapeDtypeStruct((requests, q_heads), F32),
        ),
        in_specs=[hbm] * 6,
        out_specs=(vmem, vmem),
        scratch_shapes=[
            pltpu.SMEM(positions.shape, I32),
            pltpu.SMEM(lengths.shape, I32),
            pltpu.VMEM(queries.shape, BF16),
            pltpu.VMEM(keep.shape, I32),
            pltpu.VMEM(placement.shape, I32),
            dma((5,)),
            pltpu.SMEM((8, 128), I32),
            pltpu.VMEM((8, spread * block_len), F32),
            dma,
            pltpu.VMEM(kv_cache.shape, BF16),
            pltpu.VMEM((owners, kv_heads, rows_q, head_dim), BF16),
            pltpu.VMEM((owners, 8, 128), I32),
            pltpu.VMEM((owners, 8, 128), I32),
            pltpu.SMEM((owners, 8, 128), I32),
            pltpu.VMEM((owners, spread * block_len), F32),
            pltpu.VMEM(part, F32),
            pltpu.VMEM(part, F32),
            pltpu.VMEM(part, F32),
            pltpu.VMEM((chips, kv_heads, rows_q, head_dim), BF16),
            pltpu.VMEM((chips, kv_heads, rows_q, head_dim), BF16),
            pltpu.VMEM((chips, 2 * kv_heads, rows_q), F32),
            pltpu.VMEM((chips, 2 * kv_heads, rows_q), F32),
            dma((CHUNKS,)), dma((owners,)), dma((owners,)), dma,
            dma((chips,)), dma((owners,)), dma((chips,)), dma((chips,)), dma((chips,)),
            dma((chips,)), dma((chips,)), dma((chips,)), dma((chips,)),
        ],
        compiler_params=pltpu.CompilerParams(
            collective_id=0, has_side_effects=True, vmem_limit_bytes=62 * 2 ** 20),
        name="paged",
    )(positions, lengths, queries, keep, placement, kv_cache)


def solution(mesh):
    in_specs = (
        P(("groups", "dp", "sub"), "head", None),
        P(("groups", "dp", "sub"), "head", None, None, None),
        P(("groups", "dp", "sub"), None),
        P(("groups", "dp", "sub")),
        P(("groups", "dp", "sub"), None),
        P(("groups", "dp", "sub")),
    )
    out_specs = (P(("groups", "dp", "sub"), "head", None), P(("groups", "dp", "sub"), "head"))
    return jax.shard_map(local, mesh=mesh, in_specs=in_specs, out_specs=out_specs, check_vma=False)
```

```python
from functools import partial
import math

import jax
import jax.numpy as jnp
import numpy as np
from jax import lax
from jax.experimental import pallas as pl
from jax.experimental.pallas import tpu as pltpu
from jax.sharding import PartitionSpec as P

MESH = pl.DeviceIdType.MESH
DEAD = -1e30
CHUNKS = 8
F32 = jnp.float32
BF16 = jnp.bfloat16
I32 = jnp.int32


def dot_lanes(a, b):
    return lax.dot_general(a, b, (((1,), (1,)), ((), ())), preferred_element_type=F32)


def iota(shape, axis):
    return lax.broadcasted_iota(I32, shape, axis)


def kernel(
    chips, subs, pos_hbm, len_hbm, q_hbm, keep_hbm, place_hbm, kv_ref,
    att_ref, log_ref,
    pos_ref, len_ref, q_ref, keep_ref, place_ref, in_sem, own_s, own_live, own_sem, kv, qall, meta_send, meta_recv, meta_s, live_of, own, sib_send, sib_recv, z_send, z_recv, zs_send, zs_recv,
    kv_sem, meta_ssem, meta_rsem, smem_sem, q_ssem, q_rsem, relay_ssem, sib_ssem, sib_rsem,
    z_ssem, z_rsem, zs_ssem, zs_rsem,
):
    owners = chips * subs
    requests, q_heads, head_dim = q_ref.shape
    pool, kv_heads, _, block_len, _ = kv_ref.shape
    group = q_heads // kv_heads
    blocks = place_ref.shape[1]
    kept = keep_ref.shape[1]
    spread = pool // owners
    rows_q = requests * group
    half = head_dim // 2
    scale = head_dim ** -0.5 * math.log2(math.e)
    shift = pool.bit_length() - 1
    my_chip = lax.axis_index("dp")
    my_sub = lax.axis_index("sub")
    me = my_chip * subs + my_sub
    other = 1 - my_sub

    def place(o):
        return {"dp": o // subs, "sub": lax.rem(o, subs)}

    def kv_copy(i):
        part = pl.ds(i * (pool // CHUNKS), pool // CHUNKS)
        return pltpu.make_async_copy(kv_ref.at[part], kv.at[part], kv_sem.at[i])

    def meta_copy(o, slot):
        return pltpu.make_async_remote_copy(
            src_ref=meta_send.at[o], dst_ref=meta_recv.at[slot], send_sem=meta_ssem.at[o],
            recv_sem=meta_rsem.at[slot], device_id=place(o), device_id_type=MESH)

    def q_copy(to, slot, ssem):
        return pltpu.make_async_remote_copy(
            src_ref=qall.at[slot], dst_ref=qall.at[slot], send_sem=ssem,
            recv_sem=q_rsem.at[slot], device_id=place(to), device_id_type=MESH)

    def sib_copy(t):
        return pltpu.make_async_remote_copy(
            src_ref=sib_send.at[t], dst_ref=sib_recv.at[t], send_sem=sib_ssem.at[t],
            recv_sem=sib_rsem.at[t], device_id=place(my_chip * subs + other), device_id_type=MESH)

    def z_copies(t, chip, slot):
        to = place(chip * subs + my_sub)
        return (
            pltpu.make_async_remote_copy(
                src_ref=z_send.at[t], dst_ref=z_recv.at[slot], send_sem=z_ssem.at[t],
                recv_sem=z_rsem.at[slot], device_id=to, device_id_type=MESH),
            pltpu.make_async_remote_copy(
                src_ref=zs_send.at[t], dst_ref=zs_recv.at[slot], send_sem=zs_ssem.at[t],
                recv_sem=zs_rsem.at[slot], device_id=to, device_id_type=MESH),
        )

    inputs = [
        pltpu.make_async_copy(source, here, in_sem.at[i])
        for i, (source, here) in enumerate((
            (place_hbm, place_ref), (keep_hbm, keep_ref), (len_hbm, len_ref), (pos_hbm, pos_ref), (q_hbm, q_ref)))
    ]
    for copy in inputs:
        copy.start()

    barrier = pltpu.get_barrier_semaphore()

    @pl.loop(1, owners)
    def _(i):
        pl.semaphore_signal(barrier, inc=1, device_id=place(lax.rem(me + i, owners)), device_id_type=MESH)

    for i in range(CHUNKS):
        kv_copy(i).start()

    for copy in inputs:
        copy.wait()

    row = iota((requests, 1), 0)
    positions = jnp.zeros((requests, 1), F32)
    for r in range(requests):
        positions = jnp.where(row == r, pos_ref[r].astype(F32), positions)
    place_i = iota((1, half), 1)
    freq = jnp.ones((1, half), F32)
    for bit in range(half.bit_length() - 1):
        step = float(np.float32(1000000.0 ** (-2.0 * 2 ** bit / head_dim)))
        freq = freq * jnp.where((place_i & (1 << bit)) != 0, step, 1.0)
    angle = positions * freq
    cosine, sine = jnp.cos(angle)[:, None, :], jnp.sin(angle)[:, None, :]
    values = q_ref[...].astype(F32)
    first, second = values[..., :half], values[..., half:]
    rotated = jnp.concatenate([first * cosine - second * sine, second * cosine + first * sine], axis=-1)
    for k in range(kv_heads):
        qall[me, k] = rotated[:, k * group:(k + 1) * group, :].reshape(rows_q, head_dim).astype(BF16)

    table = place_ref[...]
    owner_of = lax.shift_right_logical(table, shift)
    local_of = table & (pool - 1)
    low, high = (local_of & 255).astype(F32), lax.shift_right_logical(local_of, 8).astype(F32)
    member = [
        (owner_of[r:r + 1] == iota((owners, blocks), 0)).astype(F32) for r in range(requests)
    ]
    before = (iota((blocks, blocks), 0) < iota((blocks, blocks), 1)).astype(F32).astype(BF16)
    ranks = jnp.dot(jnp.concatenate(member, 0).astype(BF16), before, preferred_element_type=F32)
    base = jnp.zeros((owners, 1), F32)
    fields = jnp.zeros((3 * owners, spread), F32)
    for r in range(requests):
        m = member[r]
        rank = jnp.sum(m * (ranks[r * owners:(r + 1) * owners] + base), axis=0, keepdims=True)
        base = base + jnp.sum(m, axis=1, keepdims=True)
        at = (rank.astype(I32) == iota((spread, blocks), 0)).astype(F32).astype(BF16)
        named = (keep_ref[r:r + 1, :] == iota((blocks, kept), 0)).astype(F32).astype(BF16)
        live = jnp.clip(len_ref[r] - iota((8, kept), 1) * block_len, 0, block_len)
        count = dot_lanes(live.astype(F32).astype(BF16), named)[:1]
        code = count + float(r * (block_len + 1))
        stacked = jnp.concatenate([m * low[r:r + 1], m * high[r:r + 1], m * code], 0)
        fields = fields + dot_lanes(stacked.astype(BF16), at)
    ids = (fields[:owners] + 256.0 * fields[owners:2 * owners]).astype(I32)
    codes = fields[2 * owners:].astype(I32)
    meta_send[...] = jnp.zeros_like(meta_send)
    for o in range(owners):
        meta_send[o, 0:1, 0:spread] = ids[o:o + 1]
        meta_send[o, 1:2, 0:spread] = codes[o:o + 1]
    meta_recv[me] = meta_send[me]

    own_smem = pltpu.make_async_copy(meta_send.at[me], own_s, own_sem)
    own_smem.start()
    keys = spread * block_len
    expand = (lax.shift_right_logical(iota((spread, keys), 1), block_len.bit_length() - 1)
              == iota((spread, keys), 0)).astype(F32).astype(BF16)

    def live_requests(codes):
        wide = jnp.dot(codes.astype(F32).astype(BF16), expand, preferred_element_type=F32)
        request = jnp.floor((wide + 0.5) * (1.0 / (block_len + 1)))
        count = wide - request * (block_len + 1)
        token = (iota(wide.shape, 1) & (block_len - 1)).astype(F32)
        return jnp.where(token < count, request, -1.0)

    own_live[...] = live_requests(jnp.broadcast_to(meta_send[me, 1:2, 0:spread], (8, spread)))
    own_smem.wait()

    pl.semaphore_wait(barrier, owners - 1)

    @pl.loop(1, owners)
    def _(i):
        o = lax.rem(me + i, owners)
        meta_copy(o, me).start()

    q_copy(my_chip * subs + other, me, q_ssem.at[0]).start()

    @pl.loop(1, chips)
    def _(t):
        chip = lax.rem(my_chip + t, chips)
        q_copy(chip * subs + my_sub, me, q_ssem.at[t]).start()

    for i in range(CHUNKS):
        kv_copy(i).wait()

    lane = iota((rows_q, head_dim), 1)

    def attend(o, live, rows, out):
        wanted = jnp.broadcast_to(live, (group, keys))
        ids = [rows[0, j] & (pool - 1) for j in range(spread)]
        stats = jnp.zeros((rows_q, head_dim), F32)
        scores, weights = [], []
        for k in range(kv_heads):
            key = jnp.concatenate([kv[ids[j], k, 0] for j in range(spread)], 0)
            scores.append(dot_lanes(qall[o, k], key))
        for k in range(kv_heads):
            score = jnp.concatenate(
                [jnp.where(wanted == float(r), scores[k][r * group:(r + 1) * group], DEAD) for r in range(requests)], 0)
            peak = jnp.max(score, axis=1, keepdims=True)
            weight = jnp.exp2((score - peak) * scale).astype(BF16)
            total = jnp.sum(weight.astype(F32), axis=1, keepdims=True)
            weights.append(weight)
            stats = jnp.where(lane == k, peak, stats)
            stats = jnp.where(lane == kv_heads + k, total, stats)
        parts = []
        for k in range(kv_heads):
            value = jnp.concatenate([kv[ids[j], k, 1] for j in range(spread)], 0)
            parts.append(jnp.dot(weights[k], value, preferred_element_type=F32))
        for k in range(kv_heads):
            out[k] = parts[k]
        out[kv_heads] = stats

    def merge(t):
        a, b = own[t, kv_heads], sib_recv[t, kv_heads]
        stats = jnp.zeros((rows_q, head_dim), F32)
        for k in range(kv_heads):
            ma, mb = a[:, k:k + 1], b[:, k:k + 1]
            la, lb = a[:, kv_heads + k:kv_heads + k + 1], b[:, kv_heads + k:kv_heads + k + 1]
            peak = jnp.maximum(ma, mb)
            wa, wb = jnp.exp2((ma - peak) * scale), jnp.exp2((mb - peak) * scale)
            own[t, k] = own[t, k] * wa + sib_recv[t, k] * wb
            stats = jnp.where(lane == k, peak, stats)
            stats = jnp.where(lane == kv_heads + k, la * wa + lb * wb, stats)
        own[t, kv_heads] = stats

    def send_back(t):
        sib_copy(t).wait_recv()
        merge(t)
        for k in range(kv_heads):
            z_send[t, k] = own[t, k].astype(BF16)
        zs_send[t] = jnp.transpose(own[t, kv_heads])[:2 * kv_heads]
        for copy in z_copies(t, lax.rem(my_chip + t, chips), my_chip):
            copy.start()

    attend(me, own_live[0:1, :], own_s, own.at[0])

    @pl.loop(1, owners)
    def _(i):
        o = lax.rem(me + i, owners)
        meta_copy(o, o).wait_recv()

    to_smem = pltpu.make_async_copy(meta_recv, meta_s, smem_sem)
    to_smem.start()
    live_of[...] = live_requests(meta_recv[:, 1, 0:spread])
    to_smem.wait()

    @pl.loop(0, chips)
    def _(t):
        chip = lax.rem(my_chip + t, chips)
        mine, sibs = chip * subs + my_sub, chip * subs + other

        @pl.when(t < chips - 1)
        def _():
            ahead = lax.rem(my_chip + t + 1, chips) * subs + my_sub
            relay = q_copy(my_chip * subs + other, ahead, relay_ssem.at[t + 1])
            relay.wait_recv()
            relay.start()

        q_copy(my_chip * subs + other, sibs, relay_ssem.at[t]).wait_recv()
        attend(sibs, live_of[pl.ds(sibs, 1), :], meta_s.at[sibs], sib_send.at[t])
        sib_copy(t).start()

        @pl.when(t > 0)
        def _():
            attend(mine, live_of[pl.ds(mine, 1), :], meta_s.at[mine], own.at[t])
            send_back(t)

    sib_copy(0).wait_recv()
    merge(0)

    @pl.loop(1, chips)
    def _(t):
        chip = lax.rem(my_chip + chips - t, chips)
        for copy in z_copies(t, chip, chip):
            copy.wait_recv()
        pad = jnp.zeros((head_dim - 2 * kv_heads, rows_q), F32)
        b = jnp.transpose(jnp.concatenate([zs_recv[chip], pad], 0))
        a = own[0, kv_heads]
        stats = jnp.zeros((rows_q, head_dim), F32)
        for k in range(kv_heads):
            ma, mb = a[:, k:k + 1], b[:, k:k + 1]
            la, lb = a[:, kv_heads + k:kv_heads + k + 1], b[:, kv_heads + k:kv_heads + k + 1]
            peak = jnp.maximum(ma, mb)
            wa, wb = jnp.exp2((ma - peak) * scale), jnp.exp2((mb - peak) * scale)
            own[0, k] = own[0, k] * wa + z_recv[chip, k].astype(F32) * wb
            stats = jnp.where(lane == k, peak, stats)
            stats = jnp.where(lane == kv_heads + k, la * wa + lb * wb, stats)
        own[0, kv_heads] = stats

    stats = own[0, kv_heads]
    outs = []
    spot = iota((rows_q, q_heads), 1)
    turn = iota((rows_q, q_heads), 0) & (group - 1)
    logs = jnp.zeros((rows_q, q_heads), F32)
    for k in range(kv_heads):
        norm = stats[:, kv_heads + k:kv_heads + k + 1]
        outs.append((own[0, k] / norm).reshape(requests, group, head_dim))
        value = stats[:, k:k + 1] * (head_dim ** -0.5) + jnp.log(norm)
        logs = jnp.where(spot == turn + k * group, value, logs)
    att_ref[...] = jnp.concatenate(outs, 1).astype(BF16)
    log_ref[...] = jnp.sum(logs.reshape(requests, group, q_heads), axis=1)

    @pl.loop(1, owners)
    def _(i):
        meta_copy(lax.rem(me + i, owners), me).wait_send()

    @pl.loop(0, chips)
    def _(t):
        q_copy(my_chip * subs + other, me, q_ssem.at[t]).wait_send()
        sib_copy(t).wait_send()

    @pl.loop(1, chips)
    def _(t):
        chip = lax.rem(my_chip + t, chips)
        q_copy(my_chip * subs + other, chip * subs + my_sub, relay_ssem.at[t]).wait_send()
        for copy in z_copies(t, chip, my_chip):
            copy.wait_send()


def local(queries, kv_cache, keep, lengths, placement, positions):
    chips, subs = lax.axis_size("dp"), lax.axis_size("sub")
    owners = chips * subs
    requests, q_heads, head_dim = queries.shape
    pool, kv_heads, _, block_len, _ = kv_cache.shape
    spread = pool // owners
    group = q_heads // kv_heads
    rows_q = requests * group
    assert head_dim & (head_dim - 1) == 0
    assert subs == 2 and pool & (pool - 1) == 0 and pool <= 65536
    assert requests * (block_len + 1) <= 256 and block_len & (block_len - 1) == 0
    assert 2 * kv_heads <= head_dim and group & (group - 1) == 0 and spread <= 128
    vmem, hbm = pl.BlockSpec(memory_space=pltpu.VMEM), pl.BlockSpec(memory_space=pltpu.HBM)
    dma = pltpu.SemaphoreType.DMA
    part = (chips, kv_heads + 1, rows_q, head_dim)
    return pl.pallas_call(
        partial(kernel, chips, subs),
        out_shape=(
            jax.ShapeDtypeStruct(queries.shape, BF16),
            jax.ShapeDtypeStruct((requests, q_heads), F32),
        ),
        in_specs=[hbm] * 6,
        out_specs=(vmem, vmem),
        scratch_shapes=[
            pltpu.SMEM(positions.shape, I32),
            pltpu.SMEM(lengths.shape, I32),
            pltpu.VMEM(queries.shape, BF16),
            pltpu.VMEM(keep.shape, I32),
            pltpu.VMEM(placement.shape, I32),
            dma((5,)),
            pltpu.SMEM((8, 128), I32),
            pltpu.VMEM((8, spread * block_len), F32),
            dma,
            pltpu.VMEM(kv_cache.shape, BF16),
            pltpu.VMEM((owners, kv_heads, rows_q, head_dim), BF16),
            pltpu.VMEM((owners, 8, 128), I32),
            pltpu.VMEM((owners, 8, 128), I32),
            pltpu.SMEM((owners, 8, 128), I32),
            pltpu.VMEM((owners, spread * block_len), F32),
            pltpu.VMEM(part, F32),
            pltpu.VMEM(part, F32),
            pltpu.VMEM(part, F32),
            pltpu.VMEM((chips, kv_heads, rows_q, head_dim), BF16),
            pltpu.VMEM((chips, kv_heads, rows_q, head_dim), BF16),
            pltpu.VMEM((chips, 2 * kv_heads, rows_q), F32),
            pltpu.VMEM((chips, 2 * kv_heads, rows_q), F32),
            dma((CHUNKS,)), dma((owners,)), dma((owners,)), dma,
            dma((chips,)), dma((owners,)), dma((chips,)), dma((chips,)), dma((chips,)),
            dma((chips,)), dma((chips,)), dma((chips,)), dma((chips,)),
        ],
        compiler_params=pltpu.CompilerParams(
            collective_id=0, has_side_effects=True, vmem_limit_bytes=62 * 2 ** 20),
        name="paged",
    )(positions, lengths, queries, keep, placement, kv_cache)


def solution(mesh):
    in_specs = (
        P(("groups", "dp", "sub"), "head", None),
        P(("groups", "dp", "sub"), "head", None, None, None),
        P(("groups", "dp", "sub"), None),
        P(("groups", "dp", "sub")),
        P(("groups", "dp", "sub"), None),
        P(("groups", "dp", "sub")),
    )
    out_specs = (P(("groups", "dp", "sub"), "head", None), P(("groups", "dp", "sub"), "head"))
    return jax.shard_map(local, mesh=mesh, in_specs=in_specs, out_specs=out_specs, check_vma=False)
```
